32 devices in a mesh: seq: 8 (over z, y), head: 4 (over x, core).
Axes of the slice: x: 2, y: 2, z: 4, core: 2. Of those that a mesh axis runs over, the one named last changes fastest.
Arguments:
- tokens: bfloat16 [6144, 4096], P('seq'), may hold values from -6 to 6
- w_qkv: bfloat16 [3, 4096, 4096], P(None, 'seq', 'head'), may hold values from -0.09375 to 0.09375
- w_out: bfloat16 [4096, 4096], P('head', 'seq'), may hold values from -0.09375 to 0.09375
- prior_state: float32 [32, 128, 128], P('head'), may hold values from -384 to 384
- norm_gain: float32 [4096], P('head'), may hold values from 0.1 to 1.9
Outputs:
- mixed: bfloat16 [6144, 4096], P('seq', 'head')
The draws below stay inside these ranges and needn't reach their ends.
All inputs are finite; a program needn't handle non-finite values.
Results may differ from the reference program's by a relative error of at most 0.013.
Values may be sent and summed in bfloat16 or wider, within the bound.
A program may use at most 128 MiB of HBM per device.

```python
import jax
import jax.numpy as jnp
from jax import lax

D = 4096
HEADS = 32
HEAD_DIM = 128
TOK_DEV = 768
TOKENS = 6144
N_HEAD = 4


def block_levels(stream_key, dims, cuts, least, high):
    loudness, own = 1.0, jax.random.fold_in(stream_key, 6)
    for position, parts in cuts:
        steps = jnp.exp(jax.random.uniform(jax.random.fold_in(own, position), (parts,), jnp.float32, least / len(cuts), high / len(cuts)))
        loudness = loudness * jnp.repeat(steps, dims[position] // parts).reshape([-1 if axis == position else 1 for axis in range(len(dims))])
    return loudness


def noise(stream_key, shape, deviation, bound, split=(), dtype=jnp.bfloat16):
    values = deviation * jax.random.normal(stream_key, shape, jnp.float32)
    if split:
        values = values * block_levels(stream_key, shape, split, -0.22, 0.18)
    return jnp.clip(values, -bound, bound).astype(dtype)


def setup_inputs(seed: int = 0) -> dict:
    keys = jax.random.split(jax.random.key(seed), 6)
    tokens = noise(keys[0], (TOKENS, D), 1.0, 6.0, ((0, 8),))
    w_qkv = noise(keys[1], (3, D, D), D ** -0.5, 0.09375, ((1, 8), (2, 4)))
    w_out = noise(keys[2], (D, D), D ** -0.5, 0.09375, ((0, 4), (1, 8)))
    prior_state = noise(keys[3], (HEADS, HEAD_DIM, HEAD_DIM), 64.0, 384.0, ((0, 4),), jnp.float32)
    norm_gain = jnp.clip(1.0 + 0.18 * jax.random.normal(keys[4], (D,), jnp.float32), 0.1, 1.9)
    return {"tokens": tokens, "w_qkv": w_qkv, "w_out": w_out, "prior_state": prior_state, "norm_gain": norm_gain}


def block_attend(items):
    query, key, value, prefix, gain = items
    f32 = jnp.float32
    scores = jnp.einsum('thi,shi->hts', query.astype(f32), key.astype(f32))
    place = jnp.arange(TOK_DEV)
    keep = place[None, :] <= place[:, None]
    scores = jnp.where(keep[None], scores, 0.0).astype(jnp.bfloat16)
    inner = jnp.einsum('hts,shj->thj', scores.astype(f32), value.astype(f32))
    outer = jnp.einsum('thi,hij->thj', query.astype(f32), prefix, precision=lax.Precision.HIGHEST)
    attended = inner + outer
    scale = lax.rsqrt(lax.optimization_barrier(jnp.mean(attended * attended, axis=2, keepdims=True)) + 1e-06)
    normed = attended * scale * gain
    return normed.astype(jnp.bfloat16).reshape(TOK_DEV, D)

def reference(tokens, w_qkv, w_out, prior_state, norm_gain):
    f32 = jnp.float32
    blocks = TOKENS // TOK_DEV
    shape = (blocks, TOK_DEV, HEADS, HEAD_DIM)
    query = jax.nn.silu(jnp.dot(tokens, w_qkv[0], preferred_element_type=f32)).astype(jnp.bfloat16).reshape(shape)
    key = jax.nn.silu(jnp.dot(tokens, w_qkv[1], preferred_element_type=f32)).astype(jnp.bfloat16).reshape(shape)
    value = jnp.dot(tokens, w_qkv[2], preferred_element_type=f32).astype(jnp.bfloat16).reshape(shape)
    block_state = jnp.einsum('bthi,bthj->bhij', key.astype(f32), value.astype(f32))
    prefix = prior_state[None] + jnp.cumsum(block_state, axis=0) - block_state
    gain = norm_gain.reshape(HEADS, HEAD_DIM)
    gains = jnp.broadcast_to(gain[None], (blocks, HEADS, HEAD_DIM))
    normed = lax.map(block_attend, (query, key, value, prefix, gains)).reshape(TOKENS, D)
    group = D // N_HEAD
    total = jnp.zeros((TOKENS, D), f32)
    for index in range(N_HEAD):
        partial_value = jnp.dot(normed[:, index * group:(index + 1) * group], w_out[index * group:(index + 1) * group], preferred_element_type=f32).astype(jnp.bfloat16)
        partial_value = lax.optimization_barrier(partial_value)
        total = total + partial_value.astype(f32)
    return total.astype(jnp.bfloat16)
```

```python
import functools

import jax
import jax.numpy as jnp
from jax import lax
from jax.experimental import pallas as pl
from jax.experimental.pallas import tpu as pltpu
from jax.sharding import PartitionSpec as P

HEAD_DIM = 128
MESH = pl.DeviceIdType.MESH


def gather_kernel(n, pieces, arrays, *refs):
    ins, outs = refs[:arrays], refs[arrays : 2 * arrays]
    send_sem, recv_sem, local_sem = refs[2 * arrays :]
    me = lax.axis_index("seq")
    length = n // 2
    row, side = me // 2, me % 2
    pair = row * 2 + 1 - side
    has_left, has_right = row > 0, row < length - 1
    left, right = me - 2, me + 2

    barrier = pltpu.get_barrier_semaphore()
    pl.semaphore_signal(barrier, inc=1, device_id={"seq": pair}, device_id_type=MESH)

    @pl.when(has_left)
    def _():
        pl.semaphore_signal(barrier, inc=1, device_id={"seq": left}, device_id_type=MESH)

    @pl.when(has_right)
    def _():
        pl.semaphore_signal(barrier, inc=1, device_id={"seq": right}, device_id_type=MESH)

    pl.semaphore_wait(barrier, 1 + has_left.astype(jnp.int32) + has_right.astype(jnp.int32))

    def copy(owner, piece, way, own=False):
        array, source, target, _ = pieces[piece]
        place = outs[array].at[target(owner)]
        return pltpu.make_async_remote_copy(
            src_ref=ins[array].at[source] if own else place,
            dst_ref=place,
            send_sem=send_sem.at[way, owner, piece],
            recv_sem=recv_sem.at[owner, piece],
            device_id={"seq": (left, right, pair)[way]},
            device_id_type=MESH,
        )

    def along(step, received, act):
        for piece, (_, _, _, cross) in enumerate(pieces):
            for lane in range(2 if cross else 1):
                off = side if lane == 0 else 1 - side
                for way, owner_row, there, further in (
                    (1, row - step, row >= step, has_right),
                    (0, row + step, row + step < length, has_left),
                ):
                    owner = owner_row * 2 + off

                    @pl.when(there)
                    def _():
                        if received:
                            copy(owner, piece, 2).wait_recv()
                        if not cross:
                            act(copy(owner, piece, 2))

                        @pl.when(further)
                        def _():
                            act(copy(owner, piece, way))

    def begin(act):
        for piece, (_, _, _, cross) in enumerate(pieces):
            act(copy(me, piece, 2, True))

            @pl.when(has_left)
            def _():
                act(copy(me, piece, 0, True))

            @pl.when(has_right)
            def _():
                act(copy(me, piece, 1, True))

    def crossed(received, act):
        for piece, (_, _, _, cross) in enumerate(pieces):
            if cross:
                if received:
                    copy(pair, piece, 2).wait_recv()

                @pl.when(has_left)
                def _():
                    act(copy(pair, piece, 0))

                @pl.when(has_right)
                def _():
                    act(copy(pair, piece, 1))

    locals_ = [
        pltpu.make_async_copy(
            ins[array].at[source], outs[array].at[target(me)], local_sem.at[piece]
        )
        for piece, (array, source, target, _) in enumerate(pieces)
    ]
    begin(lambda c: c.start())
    for c in locals_:
        c.start()
    crossed(True, lambda c: c.start())

    @pl.loop(1, length)
    def _(step):
        along(step, True, lambda c: c.start())

    @pl.loop(0, length)
    def _(other):
        owner = other * 2 + 1 - side
        for piece, (_, _, _, cross) in enumerate(pieces):
            if not cross:
                copy(owner, piece, 2).wait_recv()

    begin(lambda c: c.wait_send())
    for c in locals_:
        c.wait()
    crossed(False, lambda c: c.wait_send())

    @pl.loop(1, length)
    def _(step):
        along(step, False, lambda c: c.wait_send())


def gather(n, identity, pieces, shapes, *blocks):
    count = len(pieces)
    anywhere = pl.BlockSpec(memory_space=pl.ANY)
    return pl.pallas_call(
        functools.partial(gather_kernel, n, pieces, len(blocks)),
        out_shape=[jax.ShapeDtypeStruct(s, b.dtype) for s, b in zip(shapes, blocks)],
        in_specs=[anywhere] * len(blocks),
        out_specs=[anywhere] * len(blocks),
        scratch_shapes=[
            pltpu.SemaphoreType.DMA((3, n, count)),
            pltpu.SemaphoreType.DMA((n, count)),
            pltpu.SemaphoreType.DMA((count,)),
        ],
        compiler_params=pltpu.CompilerParams(collective_id=identity, has_side_effects=True),
    )(*blocks)


def gather_weights(w_qkv, w_out):
    n = lax.axis_size("seq")
    _, depth, cols = w_qkv.shape
    rows, width = w_out.shape
    half, quarter = depth // 2, rows // 4
    pieces = []

    def rows_piece(c, part, cross):
        pieces.append((
            0,
            (c, pl.ds(part * half, half)),
            lambda owner: (c, pl.ds(pl.multiple_of(owner * depth + part * half, half), half)),
            cross,
        ))

    def cols_piece(part, cross):
        span = pl.ds(part * quarter, quarter)
        pieces.append((
            1,
            (span,),
            lambda owner: (span, pl.ds(pl.multiple_of(owner * width, width), width)),
            cross,
        ))

    for c in range(3):
        for part in range(2):
            rows_piece(c, part, c == 0 and part == 0)
    for part in range(4):
        cols_piece(part, part == 0)
    shapes = ((3, n * depth, cols), (rows, n * width))
    return gather(n, 0, pieces, shapes, w_qkv, w_out)


def gather_states(states):
    n = lax.axis_size("seq")
    heads = states.shape[0]
    each = heads // 4
    pieces = [
        (
            0,
            (pl.ds(part * each, each),),
            lambda owner, part=part: (owner, pl.ds(part * each, each)),
            part == 0,
        )
        for part in range(4)
    ]
    return gather(n, 1, pieces, ((n, *states.shape),), states)[0]


def per_device(tokens, w_qkv, w_out, prior_state, norm_gain):
    f32 = jnp.float32
    rows = tokens.shape[0]
    cols = w_qkv.shape[2]
    heads = cols // HEAD_DIM
    w_all, w_out_all = gather_weights(w_qkv, w_out)
    proj = jnp.einsum("td,cde->cte", tokens, w_all, preferred_element_type=f32)
    query = jax.nn.silu(proj[0]).astype(jnp.bfloat16).reshape(rows, heads, HEAD_DIM)
    key = jax.nn.silu(proj[1]).astype(jnp.bfloat16).reshape(rows, heads, HEAD_DIM)
    value = proj[2].astype(jnp.bfloat16).reshape(rows, heads, HEAD_DIM)
    local = jnp.einsum("thi,thj->hij", key, value, preferred_element_type=f32)
    states = gather_states(local.astype(jnp.bfloat16))
    before = jnp.arange(states.shape[0]) < lax.axis_index("seq")
    earlier = jnp.sum(
        jnp.where(before[:, None, None, None], states.astype(f32), 0.0), axis=0
    )
    prefix = prior_state + earlier
    scores = jnp.einsum("thi,shi->hts", query, key, preferred_element_type=f32)
    place = jnp.arange(rows)
    keep = place[None, :] <= place[:, None]
    scores = jnp.where(keep[None], scores, 0.0).astype(jnp.bfloat16)
    inner = jnp.einsum("hts,shj->thj", scores, value, preferred_element_type=f32)
    outer = jnp.einsum("thi,hij->thj", query.astype(f32), prefix, precision=lax.Precision.HIGHEST)
    attended = inner + outer
    scale = lax.rsqrt(jnp.mean(attended * attended, axis=2, keepdims=True) + 1e-06)
    normed = (
        (attended * scale * norm_gain.reshape(heads, HEAD_DIM))
        .astype(jnp.bfloat16)
        .reshape(rows, cols)
    )
    partial_value = jnp.dot(normed, w_out_all, preferred_element_type=f32)
    return lax.psum_scatter(
        partial_value.astype(jnp.bfloat16), "head", scatter_dimension=1, tiled=True
    )


def solution(mesh):
    in_specs = (
        P("seq", None),
        P(None, "seq", "head"),
        P("head", "seq"),
        P("head", None, None),
        P("head"),
    )
    out_specs = P("seq", "head")
    return jax.shard_map(
        per_device, mesh=mesh, in_specs=in_specs, out_specs=out_specs, check_vma=False
    )
```

```python
import functools

import jax
import jax.numpy as jnp
from jax import lax
from jax.experimental import pallas as pl
from jax.experimental.pallas import tpu as pltpu
from jax.sharding import PartitionSpec as P

HEAD_DIM = 128
MESH = pl.DeviceIdType.MESH


def gather_kernel(n, pieces, arrays, *refs):
    ins, outs = refs[:arrays], refs[arrays : 2 * arrays]
    send_sem, recv_sem, local_sem = refs[2 * arrays :]
    me = lax.axis_index("seq")
    length = n // 2
    row, side = me // 2, me % 2
    pair = row * 2 + 1 - side
    has_left, has_right = row > 0, row < length - 1
    left, right = me - 2, me + 2

    barrier = pltpu.get_barrier_semaphore()
    pl.semaphore_signal(barrier, inc=1, device_id={"seq": pair}, device_id_type=MESH)

    @pl.when(has_left)
    def _():
        pl.semaphore_signal(barrier, inc=1, device_id={"seq": left}, device_id_type=MESH)

    @pl.when(has_right)
    def _():
        pl.semaphore_signal(barrier, inc=1, device_id={"seq": right}, device_id_type=MESH)

    pl.semaphore_wait(barrier, 1 + has_left.astype(jnp.int32) + has_right.astype(jnp.int32))

    def copy(owner, piece, way, own=False):
        array, source, target, _ = pieces[piece]
        place = outs[array].at[target(owner)]
        return pltpu.make_async_remote_copy(
            src_ref=ins[array].at[source] if own else place,
            dst_ref=place,
            send_sem=send_sem.at[way, owner, piece],
            recv_sem=recv_sem.at[owner, piece],
            device_id={"seq": (left, right, pair)[way]},
            device_id_type=MESH,
        )

    def along(step, received, act):
        for piece, (_, _, _, cross) in enumerate(pieces):
            for lane in range(2 if cross else 1):
                off = side if lane == 0 else 1 - side
                for way, owner_row, there, further in (
                    (1, row - step, row >= step, has_right),
                    (0, row + step, row + step < length, has_left),
                ):
                    owner = owner_row * 2 + off

                    @pl.when(there)
                    def _():
                        if received:
                            copy(owner, piece, 2).wait_recv()
                        if not cross:
                            act(copy(owner, piece, 2))

                        @pl.when(further)
                        def _():
                            act(copy(owner, piece, way))

    def begin(act):
        for piece, (_, _, _, cross) in enumerate(pieces):
            act(copy(me, piece, 2, True))

            @pl.when(has_left)
            def _():
                act(copy(me, piece, 0, True))

            @pl.when(has_right)
            def _():
                act(copy(me, piece, 1, True))

    def crossed(received, act):
        for piece, (_, _, _, cross) in enumerate(pieces):
            if cross:
                if received:
                    copy(pair, piece, 2).wait_recv()

                @pl.when(has_left)
                def _():
                    act(copy(pair, piece, 0))

                @pl.when(has_right)
                def _():
                    act(copy(pair, piece, 1))

    locals_ = [
        pltpu.make_async_copy(
            ins[array].at[source], outs[array].at[target(me)], local_sem.at[piece]
        )
        for piece, (array, source, target, _) in enumerate(pieces)
    ]
    begin(lambda c: c.start())
    for c in locals_:
        c.start()
    crossed(True, lambda c: c.start())

    @pl.loop(1, length)
    def _(step):
        along(step, True, lambda c: c.start())

    @pl.loop(0, length)
    def _(other):
        owner = other * 2 + 1 - side
        for piece, (_, _, _, cross) in enumerate(pieces):
            if not cross:
                copy(owner, piece, 2).wait_recv()

    begin(lambda c: c.wait_send())
    for c in locals_:
        c.wait()
    crossed(False, lambda c: c.wait_send())

    @pl.loop(1, length)
    def _(step):
        along(step, False, lambda c: c.wait_send())


def gather(n, identity, pieces, shapes, *blocks):
    count = len(pieces)
    anywhere = pl.BlockSpec(memory_space=pl.ANY)
    return pl.pallas_call(
        functools.partial(gather_kernel, n, pieces, len(blocks)),
        out_shape=[jax.ShapeDtypeStruct(s, b.dtype) for s, b in zip(shapes, blocks)],
        in_specs=[anywhere] * len(blocks),
        out_specs=[anywhere] * len(blocks),
        scratch_shapes=[
            pltpu.SemaphoreType.DMA((3, n, count)),
            pltpu.SemaphoreType.DMA((n, count)),
            pltpu.SemaphoreType.DMA((count,)),
        ],
        compiler_params=pltpu.CompilerParams(collective_id=identity, has_side_effects=True),
    )(*blocks)


def gather_weights(w_qkv):
    n = lax.axis_size("seq")
    _, depth, cols = w_qkv.shape
    half = depth // 2
    pieces = []

    def rows_piece(c, part, cross):
        pieces.append((
            0,
            (c, pl.ds(part * half, half)),
            lambda owner: (c, pl.ds(pl.multiple_of(owner * depth + part * half, half), half)),
            cross,
        ))

    for c in range(3):
        for part in range(2):
            rows_piece(c, part, c == 0 and part == 0)
    return gather(n, 0, pieces, ((3, n * depth, cols),), w_qkv)[0]


def gather_states(states):
    n = lax.axis_size("seq")
    heads = states.shape[0]
    each = heads // 4
    pieces = [
        (
            0,
            (pl.ds(part * each, each),),
            lambda owner, part=part: (owner, pl.ds(part * each, each)),
            part == 0,
        )
        for part in range(4)
    ]
    return gather(n, 1, pieces, ((n, *states.shape),), states)[0]


def project_kernel(n, part, normed_ref, w_ref, out_ref, core_out, core_in, far_out, far_in, *sems):
    core_send, core_recv, far_send, far_recv = sems
    chips = n // 2
    width = w_ref.shape[1] // n
    parts = width // part
    me = lax.axis_index("head")
    chip, core = me // 2, me % 2
    buddy = chip * 2 + 1 - core

    def there(turn):
        return lax.rem(chip + turn, chips)

    barrier = pltpu.get_barrier_semaphore()
    for peer in [buddy] + [there(turn) * 2 + core for turn in range(1, chips)]:
        pl.semaphore_signal(barrier, inc=1, device_id={"head": peer}, device_id_type=MESH)
    pl.semaphore_wait(barrier, chips)

    def product(group, p):
        columns = pl.ds(pl.multiple_of(group * width + p * part, part), part)
        return jnp.dot(normed_ref[...], w_ref[:, columns], preferred_element_type=jnp.float32)

    def to_core(turn, p):
        return pltpu.make_async_remote_copy(
            src_ref=core_out.at[turn, p],
            dst_ref=core_in.at[turn, p],
            send_sem=core_send.at[turn, p],
            recv_sem=core_recv.at[turn, p],
            device_id={"head": buddy},
            device_id_type=MESH,
        )

    def to_chip(turn, p):
        return pltpu.make_async_remote_copy(
            src_ref=far_out.at[turn - 1, p],
            dst_ref=far_in.at[turn - 1, p],
            send_sem=far_send.at[turn - 1, p],
            recv_sem=far_recv.at[turn - 1, p],
            device_id={"head": there(turn) * 2 + core},
            device_id_type=MESH,
        )

    for turn in [*range(1, chips), 0]:

        @pl.loop(0, parts)
        def _(p):
            core_out[turn, p] = product(there(turn) * 2 + 1 - core, p).astype(core_out.dtype)
            to_core(turn, p).start()

        @pl.loop(0, parts)
        def _(p):
            total = product(there(turn) * 2 + core, p)
            to_core(turn, p).wait_recv()
            total += core_in[turn, p].astype(jnp.float32)
            if turn:
                far_out[turn - 1, p] = total.astype(far_out.dtype)
                to_chip(turn, p).start()
            else:
                for other in range(1, chips):
                    to_chip(other, p).wait_recv()
                    total += far_in[other - 1, p].astype(jnp.float32)
                out_ref[:, pl.ds(pl.multiple_of(p * part, part), part)] = total.astype(out_ref.dtype)

    for turn in range(chips):

        @pl.loop(0, parts)
        def _(p):
            to_core(turn, p).wait_send()
            if turn:
                to_chip(turn, p).wait_send()


def project_and_sum(normed, w_out):
    n = lax.axis_size("head")
    rows, depth = normed.shape
    columns = w_out.shape[1]
    width = columns // n
    part = min(width, 256)
    chips, parts = n // 2, width // part
    near = pltpu.VMEM((chips, parts, rows, part), jnp.bfloat16)
    far = pltpu.VMEM((chips - 1, parts, rows, part), jnp.bfloat16)
    dma = pltpu.SemaphoreType.DMA
    inside = pl.BlockSpec(memory_space=pltpu.VMEM)
    return pl.pallas_call(
        functools.partial(project_kernel, n, part),
        out_shape=jax.ShapeDtypeStruct((rows, width), jnp.bfloat16),
        in_specs=[inside, inside],
        out_specs=inside,
        scratch_shapes=[
            near,
            near,
            far,
            far,
            dma((chips, parts)),
            dma((chips, parts)),
            dma((chips - 1, parts)),
            dma((chips - 1, parts)),
        ],
        compiler_params=pltpu.CompilerParams(
            collective_id=2, has_side_effects=True, vmem_limit_bytes=48 * 2**20
        ),
        cost_estimate=pl.CostEstimate(
            flops=2 * rows * depth * columns,
            bytes_accessed=2 * (rows * depth + depth * columns + rows * width),
            transcendentals=0,
        ),
    )(normed, w_out)


def per_device(tokens, w_qkv, w_out, prior_state, norm_gain):
    f32 = jnp.float32
    rows = tokens.shape[0]
    cols = w_qkv.shape[2]
    heads = cols // HEAD_DIM
    w_all = gather_weights(w_qkv)
    w_all, w_out = lax.optimization_barrier((w_all, w_out))
    w_out_all = lax.all_gather(w_out, "seq", axis=1, tiled=True)
    proj = jnp.einsum("td,cde->cte", tokens, w_all, preferred_element_type=f32)
    query = jax.nn.silu(proj[0]).astype(jnp.bfloat16).reshape(rows, heads, HEAD_DIM)
    key = jax.nn.silu(proj[1]).astype(jnp.bfloat16).reshape(rows, heads, HEAD_DIM)
    value = proj[2].astype(jnp.bfloat16).reshape(rows, heads, HEAD_DIM)
    local = jnp.einsum("thi,thj->hij", key, value, preferred_element_type=f32)
    states = gather_states(local.astype(jnp.bfloat16))
    before = jnp.arange(states.shape[0]) < lax.axis_index("seq")
    earlier = jnp.sum(
        jnp.where(before[:, None, None, None], states.astype(f32), 0.0), axis=0
    )
    prefix = prior_state + earlier
    scores = jnp.einsum("thi,shi->hts", query, key, preferred_element_type=f32)
    place = jnp.arange(rows)
    keep = place[None, :] <= place[:, None]
    scores = jnp.where(keep[None], scores, 0.0).astype(jnp.bfloat16)
    inner = jnp.einsum("hts,shj->thj", scores, value, preferred_element_type=f32)
    outer = jnp.einsum("thi,hij->thj", query.astype(f32), prefix, precision=lax.Precision.HIGHEST)
    attended = inner + outer
    scale = lax.rsqrt(jnp.mean(attended * attended, axis=2, keepdims=True) + 1e-06)
    normed = (
        (attended * scale * norm_gain.reshape(heads, HEAD_DIM))
        .astype(jnp.bfloat16)
        .reshape(rows, cols)
    )
    return project_and_sum(normed, w_out_all)


def solution(mesh):
    in_specs = (
        P("seq", None),
        P(None, "seq", "head"),
        P("head", "seq"),
        P("head", None, None),
        P("head"),
    )
    out_specs = P("seq", "head")
    return jax.shard_map(
        per_device, mesh=mesh, in_specs=in_specs, out_specs=out_specs, check_vma=False
    )
```

```python
import functools

import jax
import jax.numpy as jnp
from jax import lax
from jax.experimental import pallas as pl
from jax.experimental.pallas import tpu as pltpu
from jax.sharding import PartitionSpec as P

HEAD_DIM = 128
MESH = pl.DeviceIdType.MESH


def gather_kernel(n, pieces, arrays, *refs):
    relay(n, pieces, refs[:arrays], refs[arrays : 2 * arrays], *refs[2 * arrays :])


def weights_kernel(n, pieces, depth, tokens_ref, w_ref, w_out_ref, proj_ref, w_out_all, w_all, total, *sems):
    width = 256

    def visit(owner, first=False):
        columns = pl.ds(pl.multiple_of(owner * depth, depth), depth)
        for c in range(3):

            @pl.loop(0, w_all.shape[2] // width)
            def _(tile):
                span = pl.ds(pl.multiple_of(tile * width, width), width)
                new = jnp.dot(
                    tokens_ref[:, columns], w_all[c, columns, span], preferred_element_type=jnp.float32
                )
                total[c, :, span] = new if first else total[c, :, span] + new

    relay(n, pieces, (w_ref, w_out_ref), (w_all, w_out_all), *sems, visit=visit)
    for c in range(3):

        @pl.loop(0, w_all.shape[2] // width)
        def _(tile):
            span = pl.ds(pl.multiple_of(tile * width, width), width)
            value = total[c, :, span]
            if c < 2:
                value = value / (1.0 + jnp.exp(-value))
            proj_ref[c, :, span] = value.astype(proj_ref.dtype)


def relay(n, pieces, ins, outs, send_sem, recv_sem, local_sem, visit=None):
    me = lax.axis_index("seq")
    length = n // 2
    row, side = me // 2, me % 2
    pair = row * 2 + 1 - side
    has_left, has_right = row > 0, row < length - 1
    left, right = me - 2, me + 2

    barrier = pltpu.get_barrier_semaphore()
    pl.semaphore_signal(barrier, inc=1, device_id={"seq": pair}, device_id_type=MESH)

    @pl.when(has_left)
    def _():
        pl.semaphore_signal(barrier, inc=1, device_id={"seq": left}, device_id_type=MESH)

    @pl.when(has_right)
    def _():
        pl.semaphore_signal(barrier, inc=1, device_id={"seq": right}, device_id_type=MESH)

    pl.semaphore_wait(barrier, 1 + has_left.astype(jnp.int32) + has_right.astype(jnp.int32))

    def copy(owner, piece, way, own=False):
        array, source, target, _ = pieces[piece]
        place = outs[array].at[target(owner)]
        return pltpu.make_async_remote_copy(
            src_ref=ins[array].at[source] if own else place,
            dst_ref=place,
            send_sem=send_sem.at[way, owner, piece],
            recv_sem=recv_sem.at[owner, piece],
            device_id={"seq": (left, right, pair)[way]},
            device_id_type=MESH,
        )

    def along(step, received, act):
        for piece, (_, _, _, cross) in enumerate(pieces):
            for lane in range(2 if cross else 1):
                off = side if lane == 0 else 1 - side
                for way, owner_row, there, further in (
                    (1, row - step, row >= step, has_right),
                    (0, row + step, row + step < length, has_left),
                ):
                    owner = owner_row * 2 + off

                    @pl.when(there)
                    def _():
                        if received:
                            copy(owner, piece, 2).wait_recv()
                        if not cross:
                            act(copy(owner, piece, 2))

                        @pl.when(further)
                        def _():
                            act(copy(owner, piece, way))

    def begin(act):
        for piece, (_, _, _, cross) in enumerate(pieces):
            act(copy(me, piece, 2, True))

            @pl.when(has_left)
            def _():
                act(copy(me, piece, 0, True))

            @pl.when(has_right)
            def _():
                act(copy(me, piece, 1, True))

    def crossed(received, act):
        for piece, (_, _, _, cross) in enumerate(pieces):
            if cross:
                if received:
                    copy(pair, piece, 2).wait_recv()

                @pl.when(has_left)
                def _():
                    act(copy(pair, piece, 0))

                @pl.when(has_right)
                def _():
                    act(copy(pair, piece, 1))

    locals_ = [
        pltpu.make_async_copy(
            ins[array].at[source], outs[array].at[target(me)], local_sem.at[piece]
        )
        for piece, (array, source, target, _) in enumerate(pieces)
    ]
    begin(lambda c: c.start())
    for c in locals_:
        c.start()
    if visit:
        for c in locals_:
            c.wait()
        visit(me, True)
    crossed(True, lambda c: c.start())

    def beyond(owner):
        for array in range(len(ins)):
            for piece, (which, _, _, cross) in enumerate(pieces):
                if which == array and not cross:
                    copy(owner, piece, 2).wait_recv()
            if visit and array == 0:
                visit(owner)

    def either(step, act):
        @pl.when(row >= step)
        def _():
            act(row - step)

        @pl.when(row + step < length)
        def _():
            act(row + step)

    @pl.loop(1, length)
    def _(step):
        along(step, True, lambda c: c.start())
        if visit:
            either(step, lambda r: visit(r * 2 + side))

            @pl.when(step == 1)
            def _():
                beyond(pair)

            @pl.when(step > 1)
            def _():
                either(step - 1, lambda r: beyond(r * 2 + 1 - side))

    if visit:
        either(length - 1, lambda r: beyond(r * 2 + 1 - side))
    else:

        @pl.loop(0, length)
        def _(other):
            beyond(other * 2 + 1 - side)

    begin(lambda c: c.wait_send())
    if not visit:
        for c in locals_:
            c.wait()
    crossed(False, lambda c: c.wait_send())

    @pl.loop(1, length)
    def _(step):
        along(step, False, lambda c: c.wait_send())


def gather(n, identity, pieces, shapes, *blocks):
    count = len(pieces)
    anywhere = pl.BlockSpec(memory_space=pl.ANY)
    return pl.pallas_call(
        functools.partial(gather_kernel, n, pieces, len(blocks)),
        out_shape=[jax.ShapeDtypeStruct(s, b.dtype) for s, b in zip(shapes, blocks)],
        in_specs=[anywhere] * len(blocks),
        out_specs=[anywhere] * len(blocks),
        scratch_shapes=[
            pltpu.SemaphoreType.DMA((3, n, count)),
            pltpu.SemaphoreType.DMA((n, count)),
            pltpu.SemaphoreType.DMA((count,)),
        ],
        compiler_params=pltpu.CompilerParams(collective_id=identity, has_side_effects=True),
    )(*blocks)


def project_in(tokens, w_qkv, w_out):
    n = lax.axis_size("seq")
    _, depth, cols = w_qkv.shape
    rows, width = w_out.shape
    half, band = depth // 2, rows // 6
    pieces = []

    def rows_piece(c, part, cross):
        pieces.append((
            0,
            (c, pl.ds(part * half, half)),
            lambda owner: (c, pl.ds(pl.multiple_of(owner * depth + part * half, half), half)),
            cross,
        ))

    def cols_piece(part, cross):
        span = pl.ds(part * band, band)
        pieces.append((
            1,
            (span,),
            lambda owner: (span, pl.ds(pl.multiple_of(owner * width, width), width)),
            cross,
        ))

    for c in range(3):
        for part in range(2):
            rows_piece(c, part, c == 0 and part == 0)
    for part in range(6):
        cols_piece(part, part == 0)
    count = len(pieces)
    anywhere = pl.BlockSpec(memory_space=pl.ANY)
    inside = pl.BlockSpec(memory_space=pltpu.VMEM)
    return pl.pallas_call(
        functools.partial(weights_kernel, n, pieces, depth),
        out_shape=[
            jax.ShapeDtypeStruct((3, tokens.shape[0], cols), jnp.bfloat16),
            jax.ShapeDtypeStruct((rows, n * width), jnp.bfloat16),
        ],
        in_specs=[inside, anywhere, anywhere],
        out_specs=[inside, anywhere],
        scratch_shapes=[
            pltpu.VMEM((3, n * depth, cols), jnp.bfloat16),
            pltpu.VMEM((3, tokens.shape[0], cols), jnp.float32),
            pltpu.SemaphoreType.DMA((3, n, count)),
            pltpu.SemaphoreType.DMA((n, count)),
            pltpu.SemaphoreType.DMA((count,)),
        ],
        compiler_params=pltpu.CompilerParams(
            collective_id=0, has_side_effects=True, vmem_limit_bytes=54 * 2**20
        ),
    )(tokens, w_qkv, w_out)


def gather_states(states):
    n = lax.axis_size("seq")
    heads = states.shape[0]
    each = heads // 4
    pieces = [
        (
            0,
            (pl.ds(part * each, each),),
            lambda owner, part=part: (owner, pl.ds(part * each, each)),
            part == 0,
        )
        for part in range(4)
    ]
    return gather(n, 1, pieces, ((n, *states.shape),), states)[0]


def project_kernel(n, part, normed_ref, w_ref, late_ref, out_ref, core_out, core_in, far_out, far_in, *sems):
    core_send, core_recv, far_send, far_recv = sems
    chips = n // 2
    width = w_ref.shape[1] // n
    parts = width // part
    me = lax.axis_index("head")
    chip, core = me // 2, me % 2
    buddy = chip * 2 + 1 - core

    def there(turn):
        return lax.rem(chip + turn, chips)

    barrier = pltpu.get_barrier_semaphore()
    for peer in [buddy] + [there(turn) * 2 + core for turn in range(1, chips)]:
        pl.semaphore_signal(barrier, inc=1, device_id={"head": peer}, device_id_type=MESH)
    pl.semaphore_wait(barrier, chips)

    def product(group, p):
        columns = pl.ds(pl.multiple_of(group * width + p * part, part), part)
        early = w_ref.shape[0]
        return jnp.dot(
            normed_ref[:, :early], w_ref[:, columns], preferred_element_type=jnp.float32
        ) + jnp.dot(normed_ref[:, early:], late_ref[:, columns], preferred_element_type=jnp.float32)

    def to_core(turn, p):
        return pltpu.make_async_remote_copy(
            src_ref=core_out.at[turn, p],
            dst_ref=core_in.at[turn, p],
            send_sem=core_send.at[turn, p],
            recv_sem=core_recv.at[turn, p],
            device_id={"head": buddy},
            device_id_type=MESH,
        )

    def to_chip(turn, p):
        return pltpu.make_async_remote_copy(
            src_ref=far_out.at[turn - 1, p],
            dst_ref=far_in.at[turn - 1, p],
            send_sem=far_send.at[turn - 1, p],
            recv_sem=far_recv.at[turn - 1, p],
            device_id={"head": there(turn) * 2 + core},
            device_id_type=MESH,
        )

    for turn in [*range(1, chips), 0]:

        @pl.loop(0, parts)
        def _(p):
            core_out[turn, p] = product(there(turn) * 2 + 1 - core, p).astype(core_out.dtype)
            to_core(turn, p).start()

        @pl.loop(0, parts)
        def _(p):
            total = product(there(turn) * 2 + core, p)
            to_core(turn, p).wait_recv()
            total += core_in[turn, p].astype(jnp.float32)
            if turn:
                far_out[turn - 1, p] = total.astype(far_out.dtype)
                to_chip(turn, p).start()
            else:
                for other in range(1, chips):
                    to_chip(other, p).wait_recv()
                    total += far_in[other - 1, p].astype(jnp.float32)
                out_ref[:, pl.ds(pl.multiple_of(p * part, part), part)] = total.astype(out_ref.dtype)

    for turn in range(chips):

        @pl.loop(0, parts)
        def _(p):
            to_core(turn, p).wait_send()
            if turn:
                to_chip(turn, p).wait_send()


def project_and_sum(normed, w_early, w_late):
    n = lax.axis_size("head")
    rows, depth = normed.shape
    columns = w_early.shape[1]
    width = columns // n
    part = min(width, 256)
    chips, parts = n // 2, width // part
    near = pltpu.VMEM((chips, parts, rows, part), jnp.bfloat16)
    far = pltpu.VMEM((chips - 1, parts, rows, part), jnp.bfloat16)
    dma = pltpu.SemaphoreType.DMA
    inside = pl.BlockSpec(memory_space=pltpu.VMEM)
    return pl.pallas_call(
        functools.partial(project_kernel, n, part),
        out_shape=jax.ShapeDtypeStruct((rows, width), jnp.bfloat16),
        in_specs=[inside, inside, inside],
        out_specs=inside,
        scratch_shapes=[
            near,
            near,
            far,
            far,
            dma((chips, parts)),
            dma((chips, parts)),
            dma((chips - 1, parts)),
            dma((chips - 1, parts)),
        ],
        compiler_params=pltpu.CompilerParams(
            collective_id=2, has_side_effects=True, vmem_limit_bytes=48 * 2**20
        ),
        cost_estimate=pl.CostEstimate(
            flops=2 * rows * depth * columns,
            bytes_accessed=2 * (rows * depth + depth * columns + rows * width),
            transcendentals=0,
        ),
    )(normed, w_early, w_late)


def per_device(tokens, w_qkv, w_out, prior_state, norm_gain):
    f32 = jnp.float32
    rows = tokens.shape[0]
    cols = w_qkv.shape[2]
    heads = cols // HEAD_DIM
    early = w_out.shape[0] * 3 // 4
    proj, w_early = project_in(tokens, w_qkv, w_out[:early])
    proj, w_late = lax.optimization_barrier((proj, w_out[early:]))
    w_late = lax.all_gather(w_late, "seq", axis=1, tiled=True)
    query, key, value = (proj[c].reshape(rows, heads, HEAD_DIM) for c in range(3))
    local = jnp.einsum("thi,thj->hij", key, value, preferred_element_type=f32)
    states = gather_states(local.astype(jnp.bfloat16))
    before = jnp.arange(states.shape[0]) < lax.axis_index("seq")
    earlier = jnp.sum(
        jnp.where(before[:, None, None, None], states.astype(f32), 0.0), axis=0
    )
    prefix = prior_state + earlier
    scores = jnp.einsum("thi,shi->hts", query, key, preferred_element_type=f32)
    place = jnp.arange(rows)
    keep = place[None, :] <= place[:, None]
    scores = jnp.where(keep[None], scores, 0.0).astype(jnp.bfloat16)
    inner = jnp.einsum("hts,shj->thj", scores, value, preferred_element_type=f32)
    outer = jnp.einsum("thi,hij->thj", query.astype(f32), prefix, precision=lax.Precision.HIGHEST)
    attended = inner + outer
    scale = lax.rsqrt(jnp.mean(attended * attended, axis=2, keepdims=True) + 1e-06)
    normed = (
        (attended * scale * norm_gain.reshape(heads, HEAD_DIM))
        .astype(jnp.bfloat16)
        .reshape(rows, cols)
    )
    return project_and_sum(normed, w_early, w_late)


def solution(mesh):
    in_specs = (
        P("seq", None),
        P(None, "seq", "head"),
        P("head", "seq"),
        P("head", None, None),
        P("head"),
    )
    out_specs = P("seq", "head")
    return jax.shard_map(
        per_device, mesh=mesh, in_specs=in_specs, out_specs=out_specs, check_vma=False
    )
```

```python
import functools

import jax
import jax.numpy as jnp
from jax import lax
from jax.experimental import pallas as pl
from jax.experimental.pallas import tpu as pltpu
from jax.sharding import PartitionSpec as P

HEAD_DIM = 128
MESH = pl.DeviceIdType.MESH


def gather_kernel(n, pieces, arrays, *refs):
    relay(n, pieces, refs[:arrays], refs[arrays : 2 * arrays], *refs[2 * arrays :])


def weights_kernel(n, pieces, depth, tokens_ref, w_ref, w_out_ref, query_ref, key_ref, value_ref, w_out_all, w_all, total, *sems):
    width = 256

    def visit(owner, first=False):
        columns = pl.ds(pl.multiple_of(owner * depth, depth), depth)
        for c in range(3):

            @pl.loop(0, w_all.shape[2] // width)
            def _(tile):
                span = pl.ds(pl.multiple_of(tile * width, width), width)
                new = jnp.dot(
                    tokens_ref[:, columns], w_all[c, columns, span], preferred_element_type=jnp.float32
                )
                total[c, :, span] = new if first else total[c, :, span] + new

    relay(n, pieces, (w_ref, w_out_ref), (w_all, w_out_all), *sems, visit=visit)
    for c in range(3):

        @pl.loop(0, w_all.shape[2] // width)
        def _(tile):
            span = pl.ds(pl.multiple_of(tile * width, width), width)
            value = total[c, :, span]
            if c < 2:
                value = value / (1.0 + jnp.exp(-value))
            for part in range(width // HEAD_DIM):
                block = value[:, part * HEAD_DIM : (part + 1) * HEAD_DIM]
                head = tile * (width // HEAD_DIM) + part
                (query_ref, key_ref, value_ref)[c][head] = block.astype(query_ref.dtype)


def relay(n, pieces, ins, outs, send_sem, recv_sem, local_sem, visit=None):
    me = lax.axis_index("seq")
    length = n // 2
    row, side = me // 2, me % 2
    pair = row * 2 + 1 - side
    has_left, has_right = row > 0, row < length - 1
    left, right = me - 2, me + 2

    barrier = pltpu.get_barrier_semaphore()
    pl.semaphore_signal(barrier, inc=1, device_id={"seq": pair}, device_id_type=MESH)

    @pl.when(has_left)
    def _():
        pl.semaphore_signal(barrier, inc=1, device_id={"seq": left}, device_id_type=MESH)

    @pl.when(has_right)
    def _():
        pl.semaphore_signal(barrier, inc=1, device_id={"seq": right}, device_id_type=MESH)

    pl.semaphore_wait(barrier, 1 + has_left.astype(jnp.int32) + has_right.astype(jnp.int32))

    def copy(owner, piece, way, own=False):
        array, source, target, _ = pieces[piece]
        place = outs[array].at[target(owner)]
        return pltpu.make_async_remote_copy(
            src_ref=ins[array].at[source] if own else place,
            dst_ref=place,
            send_sem=send_sem.at[way, owner, piece],
            recv_sem=recv_sem.at[owner, piece],
            device_id={"seq": (left, right, pair)[way]},
            device_id_type=MESH,
        )

    def along(step, received, act):
        for piece, (_, _, _, cross) in enumerate(pieces):
            for lane in range(2 if cross else 1):
                off = side if lane == 0 else 1 - side
                for way, owner_row, there, further in (
                    (1, row - step, row >= step, has_right),
                    (0, row + step, row + step < length, has_left),
                ):
                    owner = owner_row * 2 + off

                    @pl.when(there)
                    def _():
                        if received:
                            copy(owner, piece, 2).wait_recv()
                        if not cross:
                            act(copy(owner, piece, 2))

                        @pl.when(further)
                        def _():
                            act(copy(owner, piece, way))

    def begin(act):
        for piece, (_, _, _, cross) in enumerate(pieces):
            act(copy(me, piece, 2, True))

            @pl.when(has_left)
            def _():
                act(copy(me, piece, 0, True))

            @pl.when(has_right)
            def _():
                act(copy(me, piece, 1, True))

    def crossed(received, act):
        for piece, (_, _, _, cross) in enumerate(pieces):
            if cross:
                if received:
                    copy(pair, piece, 2).wait_recv()

                @pl.when(has_left)
                def _():
                    act(copy(pair, piece, 0))

                @pl.when(has_right)
                def _():
                    act(copy(pair, piece, 1))

    locals_ = [
        pltpu.make_async_copy(
            ins[array].at[source], outs[array].at[target(me)], local_sem.at[piece]
        )
        for piece, (array, source, target, _) in enumerate(pieces)
    ]
    begin(lambda c: c.start())
    for c in locals_:
        c.start()
    if visit:
        for c in locals_:
            c.wait()
        visit(me, True)
    crossed(True, lambda c: c.start())

    def beyond(owner):
        for array in range(len(ins)):
            for piece, (which, _, _, cross) in enumerate(pieces):
                if which == array and not cross:
                    copy(owner, piece, 2).wait_recv()
            if visit and array == 0:
                visit(owner)

    def either(step, act):
        @pl.when(row >= step)
        def _():
            act(row - step)

        @pl.when(row + step < length)
        def _():
            act(row + step)

    @pl.loop(1, length)
    def _(step):
        along(step, True, lambda c: c.start())
        if visit:
            either(step, lambda r: visit(r * 2 + side))

            @pl.when(step == 1)
            def _():
                beyond(pair)

            @pl.when(step > 1)
            def _():
                either(step - 1, lambda r: beyond(r * 2 + 1 - side))

    if visit:
        either(length - 1, lambda r: beyond(r * 2 + 1 - side))
    else:

        @pl.loop(0, length)
        def _(other):
            beyond(other * 2 + 1 - side)

    begin(lambda c: c.wait_send())
    if not visit:
        for c in locals_:
            c.wait()
    crossed(False, lambda c: c.wait_send())

    @pl.loop(1, length)
    def _(step):
        along(step, False, lambda c: c.wait_send())


def gather(n, identity, pieces, shapes, *blocks):
    count = len(pieces)
    anywhere = pl.BlockSpec(memory_space=pl.ANY)
    return pl.pallas_call(
        functools.partial(gather_kernel, n, pieces, len(blocks)),
        out_shape=[jax.ShapeDtypeStruct(s, b.dtype) for s, b in zip(shapes, blocks)],
        in_specs=[anywhere] * len(blocks),
        out_specs=[anywhere] * len(blocks),
        scratch_shapes=[
            pltpu.SemaphoreType.DMA((3, n, count)),
            pltpu.SemaphoreType.DMA((n, count)),
            pltpu.SemaphoreType.DMA((count,)),
        ],
        compiler_params=pltpu.CompilerParams(collective_id=identity, has_side_effects=True),
    )(*blocks)


def project_in(tokens, w_qkv, w_out, early):
    n = lax.axis_size("seq")
    _, depth, cols = w_qkv.shape
    width = w_out.shape[1]
    half, band = depth // 2, early // 4
    pieces = []

    def rows_piece(c, part, cross):
        pieces.append((
            0,
            (c, pl.ds(part * half, half)),
            lambda owner: (c, pl.ds(pl.multiple_of(owner * depth + part * half, half), half)),
            cross,
        ))

    def cols_piece(part, cross):
        span = pl.ds(part * band, band)
        pieces.append((
            1,
            (span,),
            lambda owner: (span, pl.ds(pl.multiple_of(owner * width, width), width)),
            cross,
        ))

    for c in range(3):
        for part in range(2):
            rows_piece(c, part, c == 0 and part == 0)
    for part in range(4):
        cols_piece(part, part == 0)
    count = len(pieces)
    anywhere = pl.BlockSpec(memory_space=pl.ANY)
    inside = pl.BlockSpec(memory_space=pltpu.VMEM)
    return pl.pallas_call(
        functools.partial(weights_kernel, n, pieces, depth),
        out_shape=[
            *[jax.ShapeDtypeStruct((cols // HEAD_DIM, tokens.shape[0], HEAD_DIM), jnp.bfloat16)] * 3,
            jax.ShapeDtypeStruct((early, n * width), jnp.bfloat16),
        ],
        in_specs=[inside, anywhere, anywhere],
        out_specs=[inside, inside, inside, anywhere],
        scratch_shapes=[
            pltpu.VMEM((3, n * depth, cols), jnp.bfloat16),
            pltpu.VMEM((3, tokens.shape[0], cols), jnp.float32),
            pltpu.SemaphoreType.DMA((3, n, count)),
            pltpu.SemaphoreType.DMA((n, count)),
            pltpu.SemaphoreType.DMA((count,)),
        ],
        compiler_params=pltpu.CompilerParams(
            collective_id=0, has_side_effects=True, vmem_limit_bytes=54 * 2**20
        ),
    )(tokens, w_qkv, w_out)


def gather_states(states):
    n = lax.axis_size("seq")
    heads = states.shape[0]
    each = heads // 4
    pieces = [
        (
            0,
            (pl.ds(part * each, each),),
            lambda owner, part=part: (owner, pl.ds(part * each, each)),
            part == 0,
        )
        for part in range(4)
    ]
    return gather(n, 1, pieces, ((n, *states.shape),), states)[0]


def project_kernel(n, part, normed_ref, w_ref, late_ref, out_ref, core_out, core_in, far_out, far_in, *sems):
    core_send, core_recv, far_send, far_recv = sems
    chips = n // 2
    width = w_ref.shape[1] // n
    parts = width // part
    me = lax.axis_index("head")
    chip, core = me // 2, me % 2
    buddy = chip * 2 + 1 - core

    def there(turn):
        return lax.rem(chip + turn, chips)

    barrier = pltpu.get_barrier_semaphore()
    for peer in [buddy] + [there(turn) * 2 + core for turn in range(1, chips)]:
        pl.semaphore_signal(barrier, inc=1, device_id={"head": peer}, device_id_type=MESH)
    pl.semaphore_wait(barrier, chips)

    def product(group, p):
        columns = pl.ds(pl.multiple_of(group * width + p * part, part), part)
        early = w_ref.shape[0]
        return jnp.dot(
            normed_ref[:, :early], w_ref[:, columns], preferred_element_type=jnp.float32
        ) + jnp.dot(normed_ref[:, early:], late_ref[:, columns], preferred_element_type=jnp.float32)

    def to_core(turn, p):
        return pltpu.make_async_remote_copy(
            src_ref=core_out.at[turn, p],
            dst_ref=core_in.at[turn, p],
            send_sem=core_send.at[turn, p],
            recv_sem=core_recv.at[turn, p],
            device_id={"head": buddy},
            device_id_type=MESH,
        )

    def to_chip(turn, p):
        return pltpu.make_async_remote_copy(
            src_ref=far_out.at[turn - 1, p],
            dst_ref=far_in.at[turn - 1, p],
            send_sem=far_send.at[turn - 1, p],
            recv_sem=far_recv.at[turn - 1, p],
            device_id={"head": there(turn) * 2 + core},
            device_id_type=MESH,
        )

    for turn in [*range(1, chips), 0]:

        @pl.loop(0, parts)
        def _(p):
            core_out[turn, p] = product(there(turn) * 2 + 1 - core, p).astype(core_out.dtype)
            to_core(turn, p).start()

        @pl.loop(0, parts)
        def _(p):
            total = product(there(turn) * 2 + core, p)
            to_core(turn, p).wait_recv()
            total += core_in[turn, p].astype(jnp.float32)
            if turn:
                far_out[turn - 1, p] = total.astype(far_out.dtype)
                to_chip(turn, p).start()
            else:
                for other in range(1, chips):
                    to_chip(other, p).wait_recv()
                    total += far_in[other - 1, p].astype(jnp.float32)
                out_ref[:, pl.ds(pl.multiple_of(p * part, part), part)] = total.astype(out_ref.dtype)

    for turn in range(chips):

        @pl.loop(0, parts)
        def _(p):
            to_core(turn, p).wait_send()
            if turn:
                to_chip(turn, p).wait_send()


def project_and_sum(normed, w_early, w_late):
    n = lax.axis_size("head")
    rows, depth = normed.shape
    columns = w_early.shape[1]
    width = columns // n
    part = min(width, 256)
    chips, parts = n // 2, width // part
    near = pltpu.VMEM((chips, parts, rows, part), jnp.bfloat16)
    far = pltpu.VMEM((chips - 1, parts, rows, part), jnp.bfloat16)
    dma = pltpu.SemaphoreType.DMA
    inside = pl.BlockSpec(memory_space=pltpu.VMEM)
    return pl.pallas_call(
        functools.partial(project_kernel, n, part),
        out_shape=jax.ShapeDtypeStruct((rows, width), jnp.bfloat16),
        in_specs=[inside, inside, inside],
        out_specs=inside,
        scratch_shapes=[
            near,
            near,
            far,
            far,
            dma((chips, parts)),
            dma((chips, parts)),
            dma((chips - 1, parts)),
            dma((chips - 1, parts)),
        ],
        compiler_params=pltpu.CompilerParams(
            collective_id=2, has_side_effects=True, vmem_limit_bytes=48 * 2**20
        ),
        cost_estimate=pl.CostEstimate(
            flops=2 * rows * depth * columns,
            bytes_accessed=2 * (rows * depth + depth * columns + rows * width),
            transcendentals=0,
        ),
    )(normed, w_early, w_late)


def per_device(tokens, w_qkv, w_out, prior_state, norm_gain):
    f32 = jnp.float32
    rows = tokens.shape[0]
    cols = w_qkv.shape[2]
    heads = cols // HEAD_DIM
    early = w_out.shape[0] // 2
    query, key, value, w_early = project_in(tokens, w_qkv, w_out, early)
    query, w_late = lax.optimization_barrier((query, w_out[early:]))
    w_late = lax.all_gather(w_late, "seq", axis=1, tiled=True)
    local = jnp.einsum("hti,htj->hij", key, value, preferred_element_type=f32)
    states = gather_states(local.astype(jnp.bfloat16))
    before = jnp.arange(states.shape[0]) < lax.axis_index("seq")
    earlier = jnp.sum(
        jnp.where(before[:, None, None, None], states.astype(f32), 0.0), axis=0
    )
    prefix = prior_state + earlier
    scores = jnp.einsum("hti,hsi->hts", query, key, preferred_element_type=f32)
    place = jnp.arange(rows)
    keep = place[None, :] <= place[:, None]
    scores = jnp.where(keep[None], scores, 0.0).astype(jnp.bfloat16)
    inner = jnp.einsum("hts,hsj->htj", scores, value, preferred_element_type=f32)
    outer = jnp.einsum("hti,hij->htj", query.astype(f32), prefix, precision=lax.Precision.HIGHEST)
    attended = inner + outer
    scale = lax.rsqrt(jnp.mean(attended * attended, axis=2, keepdims=True) + 1e-06)
    normed = (
        (attended * scale * norm_gain.reshape(heads, 1, HEAD_DIM))
        .astype(jnp.bfloat16)
        .transpose(1, 0, 2)
        .reshape(rows, cols)
    )
    return project_and_sum(normed, w_early, w_late)


def solution(mesh):
    in_specs = (
        P("seq", None),
        P(None, "seq", "head"),
        P("head", "seq"),
        P("head", None, None),
        P("head"),
    )
    out_specs = P("seq", "head")
    return jax.shard_map(
        per_device, mesh=mesh, in_specs=in_specs, out_specs=out_specs, check_vma=False
    )
```

```python
import functools

import jax
import jax.numpy as jnp
from jax import lax
from jax.experimental import pallas as pl
from jax.experimental.pallas import tpu as pltpu
from jax.sharding import PartitionSpec as P

HEAD_DIM = 128
MESH = pl.DeviceIdType.MESH


def weights_kernel(n, pieces, depth, tokens_ref, w_ref, w_out_ref, query_ref, key_ref, value_ref, w_out_all, w_all, total, *sems):
    width = 256

    def visit(owner, first=False):
        columns = pl.ds(pl.multiple_of(owner * depth, depth), depth)
        for c in range(3):

            @pl.loop(0, w_all.shape[2] // width)
            def _(tile):
                span = pl.ds(pl.multiple_of(tile * width, width), width)
                new = jnp.dot(
                    tokens_ref[:, columns], w_all[c, columns, span], preferred_element_type=jnp.float32
                )
                total[c, :, span] = new if first else total[c, :, span] + new

    relay(n, pieces, (w_ref, w_out_ref), (w_all, w_out_all), *sems, visit=visit)
    for c in range(3):

        @pl.loop(0, w_all.shape[2] // width)
        def _(tile):
            span = pl.ds(pl.multiple_of(tile * width, width), width)
            value = total[c, :, span]
            if c < 2:
                value = value / (1.0 + jnp.exp(-value))
            for part in range(width // HEAD_DIM):
                block = value[:, part * HEAD_DIM : (part + 1) * HEAD_DIM]
                head = tile * (width // HEAD_DIM) + part
                (query_ref, key_ref, value_ref)[c][head] = block.astype(query_ref.dtype)


def relay(n, pieces, ins, outs, send_sem, recv_sem, local_sem, visit=None):
    me = lax.axis_index("seq")
    length = n // 2
    row, side = me // 2, me % 2
    pair = row * 2 + 1 - side
    has_left, has_right = row > 0, row < length - 1
    left, right = me - 2, me + 2

    barrier = pltpu.get_barrier_semaphore()
    pl.semaphore_signal(barrier, inc=1, device_id={"seq": pair}, device_id_type=MESH)

    @pl.when(has_left)
    def _():
        pl.semaphore_signal(barrier, inc=1, device_id={"seq": left}, device_id_type=MESH)

    @pl.when(has_right)
    def _():
        pl.semaphore_signal(barrier, inc=1, device_id={"seq": right}, device_id_type=MESH)

    pl.semaphore_wait(barrier, 1 + has_left.astype(jnp.int32) + has_right.astype(jnp.int32))

    def copy(owner, piece, way, own=False):
        array, source, target, _ = pieces[piece]
        place = outs[array].at[target(owner)]
        return pltpu.make_async_remote_copy(
            src_ref=ins[array].at[source] if own else place,
            dst_ref=place,
            send_sem=send_sem.at[way, owner, piece],
            recv_sem=recv_sem.at[owner, piece],
            device_id={"seq": (left, right, pair)[way]},
            device_id_type=MESH,
        )

    def along(step, received, act):
        for piece, (_, _, _, cross) in enumerate(pieces):
            for lane in range(2 if cross else 1):
                off = side if lane == 0 else 1 - side
                for way, owner_row, there, further in (
                    (1, row - step, row >= step, has_right),
                    (0, row + step, row + step < length, has_left),
                ):
                    owner = owner_row * 2 + off

                    @pl.when(there)
                    def _():
                        if received:
                            copy(owner, piece, 2).wait_recv()
                        if not cross:
                            act(copy(owner, piece, 2))

                        @pl.when(further)
                        def _():
                            act(copy(owner, piece, way))

    def begin(act):
        for piece, (_, _, _, cross) in enumerate(pieces):
            act(copy(me, piece, 2, True))

            @pl.when(has_left)
            def _():
                act(copy(me, piece, 0, True))

            @pl.when(has_right)
            def _():
                act(copy(me, piece, 1, True))

    def crossed(received, act):
        for piece, (_, _, _, cross) in enumerate(pieces):
            if cross:
                if received:
                    copy(pair, piece, 2).wait_recv()

                @pl.when(has_left)
                def _():
                    act(copy(pair, piece, 0))

                @pl.when(has_right)
                def _():
                    act(copy(pair, piece, 1))

    locals_ = [
        pltpu.make_async_copy(
            ins[array].at[source], outs[array].at[target(me)], local_sem.at[piece]
        )
        for piece, (array, source, target, _) in enumerate(pieces)
    ]
    begin(lambda c: c.start())
    for c in locals_:
        c.start()
    if visit:
        for c in locals_:
            c.wait()
        visit(me, True)
    crossed(True, lambda c: c.start())

    def beyond(owner):
        for array in range(len(ins)):
            for piece, (which, _, _, cross) in enumerate(pieces):
                if which == array and not cross:
                    copy(owner, piece, 2).wait_recv()
            if visit and array == 0:
                visit(owner)

    def either(step, act):
        @pl.when(row >= step)
        def _():
            act(row - step)

        @pl.when(row + step < length)
        def _():
            act(row + step)

    @pl.loop(1, length)
    def _(step):
        along(step, True, lambda c: c.start())
        if visit:
            either(step, lambda r: visit(r * 2 + side))

            @pl.when(step == 1)
            def _():
                beyond(pair)

            @pl.when(step > 1)
            def _():
                either(step - 1, lambda r: beyond(r * 2 + 1 - side))

    if visit:
        either(length - 1, lambda r: beyond(r * 2 + 1 - side))
    else:

        @pl.loop(0, length)
        def _(other):
            beyond(other * 2 + 1 - side)

    begin(lambda c: c.wait_send())
    if not visit:
        for c in locals_:
            c.wait()
    crossed(False, lambda c: c.wait_send())

    @pl.loop(1, length)
    def _(step):
        along(step, False, lambda c: c.wait_send())


def project_in(tokens, w_qkv, w_out, early):
    n = lax.axis_size("seq")
    _, depth, cols = w_qkv.shape
    width = w_out.shape[1]
    half, band = depth // 2, early // 4
    pieces = []

    def rows_piece(c, part, cross):
        pieces.append((
            0,
            (c, pl.ds(part * half, half)),
            lambda owner: (c, pl.ds(pl.multiple_of(owner * depth + part * half, half), half)),
            cross,
        ))

    def cols_piece(part, cross):
        span = pl.ds(part * band, band)
        pieces.append((
            1,
            (span,),
            lambda owner: (span, pl.ds(pl.multiple_of(owner * width, width), width)),
            cross,
        ))

    for c in range(3):
        for part in range(2):
            rows_piece(c, part, c == 0 and part == 0)
    for part in range(4):
        cols_piece(part, part == 0)
    count = len(pieces)
    anywhere = pl.BlockSpec(memory_space=pl.ANY)
    inside = pl.BlockSpec(memory_space=pltpu.VMEM)
    return pl.pallas_call(
        functools.partial(weights_kernel, n, pieces, depth),
        out_shape=[
            *[jax.ShapeDtypeStruct((cols // HEAD_DIM, tokens.shape[0], HEAD_DIM), jnp.bfloat16)] * 3,
            jax.ShapeDtypeStruct((early, n * width), jnp.bfloat16),
        ],
        in_specs=[inside, anywhere, anywhere],
        out_specs=[inside, inside, inside, anywhere],
        scratch_shapes=[
            pltpu.VMEM((3, n * depth, cols), jnp.bfloat16),
            pltpu.VMEM((3, tokens.shape[0], cols), jnp.float32),
            pltpu.SemaphoreType.DMA((3, n, count)),
            pltpu.SemaphoreType.DMA((n, count)),
            pltpu.SemaphoreType.DMA((count,)),
        ],
        compiler_params=pltpu.CompilerParams(
            collective_id=0, has_side_effects=True, vmem_limit_bytes=54 * 2**20
        ),
    )(tokens, w_qkv, w_out)


def prefix_kernel(n, parts, local_ref, out_ref, mine, paired, came, goes, pair_send, pair_recv, line_send, line_recv):
    me = lax.axis_index("seq")
    row, side = me // 2, me % 2
    pair = row * 2 + 1 - side
    has_left, has_right = row > 0, row < n // 2 - 1
    each = local_ref.shape[0] // parts

    barrier = pltpu.get_barrier_semaphore()
    pl.semaphore_signal(barrier, inc=1, device_id={"seq": pair}, device_id_type=MESH)

    @pl.when(has_left)
    def _():
        pl.semaphore_signal(barrier, inc=1, device_id={"seq": me - 2}, device_id_type=MESH)

    @pl.when(has_right)
    def _():
        pl.semaphore_signal(barrier, inc=1, device_id={"seq": me + 2}, device_id_type=MESH)

    pl.semaphore_wait(barrier, 1 + has_left.astype(jnp.int32) + has_right.astype(jnp.int32))

    def across(p):
        span = pl.ds(p * each, each)
        return pltpu.make_async_remote_copy(
            src_ref=mine.at[span],
            dst_ref=paired.at[span],
            send_sem=pair_send.at[p],
            recv_sem=pair_recv.at[p],
            device_id={"seq": pair},
            device_id_type=MESH,
        )

    def onward(p):
        span = pl.ds(p * each, each)
        return pltpu.make_async_remote_copy(
            src_ref=goes.at[span],
            dst_ref=came.at[span],
            send_sem=line_send.at[p],
            recv_sem=line_recv.at[p],
            device_id={"seq": me + 2},
            device_id_type=MESH,
        )

    mine[...] = local_ref[...].astype(mine.dtype)
    for p in range(parts):
        across(p).start()
    out_ref[...] = jnp.zeros_like(out_ref)
    for p in range(parts):
        span = pl.ds(p * each, each)
        across(p).wait_recv()

        @pl.when(has_left)
        def _():
            onward(p).wait_recv()
            out_ref[span] = came[span].astype(jnp.float32)

        @pl.when(has_right)
        def _():
            total = out_ref[span] + local_ref[span] + paired[span].astype(jnp.float32)
            goes[span] = total.astype(goes.dtype)
            onward(p).start()

        @pl.when(side == 1)
        def _():
            out_ref[span] = out_ref[span] + paired[span].astype(jnp.float32)

    for p in range(parts):
        across(p).wait_send()

        @pl.when(has_right)
        def _():
            onward(p).wait_send()


def sum_earlier(states):
    n = lax.axis_size("seq")
    parts = 4
    inside = pl.BlockSpec(memory_space=pltpu.VMEM)
    return pl.pallas_call(
        functools.partial(prefix_kernel, n, parts),
        out_shape=jax.ShapeDtypeStruct(states.shape, jnp.float32),
        in_specs=[inside],
        out_specs=inside,
        scratch_shapes=[pltpu.VMEM(states.shape, jnp.bfloat16)] * 4
        + [pltpu.SemaphoreType.DMA((parts,))] * 4,
        compiler_params=pltpu.CompilerParams(collective_id=1, has_side_effects=True),
    )(states)


def project_kernel(n, part, normed_ref, w_ref, late_ref, out_ref, core_out, core_in, far_out, far_in, *sems):
    core_send, core_recv, far_send, far_recv = sems
    chips = n // 2
    width = w_ref.shape[1] // n
    parts = width // part
    me = lax.axis_index("head")
    chip, core = me // 2, me % 2
    buddy = chip * 2 + 1 - core

    def there(turn):
        return lax.rem(chip + turn, chips)

    barrier = pltpu.get_barrier_semaphore()
    for peer in [buddy] + [there(turn) * 2 + core for turn in range(1, chips)]:
        pl.semaphore_signal(barrier, inc=1, device_id={"head": peer}, device_id_type=MESH)
    pl.semaphore_wait(barrier, chips)

    def product(group, p):
        columns = pl.ds(pl.multiple_of(group * width + p * part, part), part)
        early = w_ref.shape[0]
        return jnp.dot(
            normed_ref[:, :early], w_ref[:, columns], preferred_element_type=jnp.float32
        ) + jnp.dot(normed_ref[:, early:], late_ref[:, columns], preferred_element_type=jnp.float32)

    def to_core(turn, p):
        return pltpu.make_async_remote_copy(
            src_ref=core_out.at[turn, p],
            dst_ref=core_in.at[turn, p],
            send_sem=core_send.at[turn, p],
            recv_sem=core_recv.at[turn, p],
            device_id={"head": buddy},
            device_id_type=MESH,
        )

    def to_chip(turn, p):
        return pltpu.make_async_remote_copy(
            src_ref=far_out.at[turn - 1, p],
            dst_ref=far_in.at[turn - 1, p],
            send_sem=far_send.at[turn - 1, p],
            recv_sem=far_recv.at[turn - 1, p],
            device_id={"head": there(turn) * 2 + core},
            device_id_type=MESH,
        )

    for turn in [*range(1, chips), 0]:

        @pl.loop(0, parts)
        def _(p):
            core_out[turn, p] = product(there(turn) * 2 + 1 - core, p).astype(core_out.dtype)
            to_core(turn, p).start()

        @pl.loop(0, parts)
        def _(p):
            total = product(there(turn) * 2 + core, p)
            to_core(turn, p).wait_recv()
            total += core_in[turn, p].astype(jnp.float32)
            if turn:
                far_out[turn - 1, p] = total.astype(far_out.dtype)
                to_chip(turn, p).start()
            else:
                for other in range(1, chips):
                    to_chip(other, p).wait_recv()
                    total += far_in[other - 1, p].astype(jnp.float32)
                out_ref[:, pl.ds(pl.multiple_of(p * part, part), part)] = total.astype(out_ref.dtype)

    for turn in range(chips):

        @pl.loop(0, parts)
        def _(p):
            to_core(turn, p).wait_send()
            if turn:
                to_chip(turn, p).wait_send()


def project_and_sum(normed, w_early, w_late):
    n = lax.axis_size("head")
    rows, depth = normed.shape
    columns = w_early.shape[1]
    width = columns // n
    part = min(width, 256)
    chips, parts = n // 2, width // part
    near = pltpu.VMEM((chips, parts, rows, part), jnp.bfloat16)
    far = pltpu.VMEM((chips - 1, parts, rows, part), jnp.bfloat16)
    dma = pltpu.SemaphoreType.DMA
    inside = pl.BlockSpec(memory_space=pltpu.VMEM)
    return pl.pallas_call(
        functools.partial(project_kernel, n, part),
        out_shape=jax.ShapeDtypeStruct((rows, width), jnp.bfloat16),
        in_specs=[inside, inside, inside],
        out_specs=inside,
        scratch_shapes=[
            near,
            near,
            far,
            far,
            dma((chips, parts)),
            dma((chips, parts)),
            dma((chips - 1, parts)),
            dma((chips - 1, parts)),
        ],
        compiler_params=pltpu.CompilerParams(
            collective_id=2, has_side_effects=True, vmem_limit_bytes=48 * 2**20
        ),
        cost_estimate=pl.CostEstimate(
            flops=2 * rows * depth * columns,
            bytes_accessed=2 * (rows * depth + depth * columns + rows * width),
            transcendentals=0,
        ),
    )(normed, w_early, w_late)


def per_device(tokens, w_qkv, w_out, prior_state, norm_gain):
    f32 = jnp.float32
    rows = tokens.shape[0]
    cols = w_qkv.shape[2]
    heads = cols // HEAD_DIM
    early = w_out.shape[0] * 3 // 4
    query, key, value, w_early = project_in(tokens, w_qkv, w_out, early)
    query, w_late = lax.optimization_barrier((query, w_out[early:]))
    w_late = lax.all_gather(w_late, "seq", axis=1, tiled=True)
    local = jnp.einsum("hti,htj->hij", key, value, preferred_element_type=f32)
    earlier = sum_earlier(local)
    prefix = prior_state + earlier
    scores = jnp.einsum("hti,hsi->hts", query, key, preferred_element_type=f32)
    place = jnp.arange(rows)
    keep = place[None, :] <= place[:, None]
    scores = jnp.where(keep[None], scores, 0.0).astype(jnp.bfloat16)
    inner = jnp.einsum("hts,hsj->htj", scores, value, preferred_element_type=f32)
    outer = jnp.einsum("hti,hij->htj", query.astype(f32), prefix, precision=lax.Precision.HIGHEST)
    attended = inner + outer
    scale = lax.rsqrt(jnp.mean(attended * attended, axis=2, keepdims=True) + 1e-06)
    normed = (
        (attended * scale * norm_gain.reshape(heads, 1, HEAD_DIM))
        .astype(jnp.bfloat16)
        .transpose(1, 0, 2)
        .reshape(rows, cols)
    )
    return project_and_sum(normed, w_early, w_late)


def solution(mesh):
    in_specs = (
        P("seq", None),
        P(None, "seq", "head"),
        P("head", "seq"),
        P("head", None, None),
        P("head"),
    )
    out_specs = P("seq", "head")
    return jax.shard_map(
        per_device, mesh=mesh, in_specs=in_specs, out_specs=out_specs, check_vma=False
    )
```
